256 devices in a mesh: region: 16 (over x, y), within: 16 (over z, core).
Axes of the slice: x: 4, y: 4, z: 8, core: 2. Of those that a mesh axis runs over, the one named last changes fastest.
Arguments:
- kernel_tiles: bfloat16 [8192, 5, 128, 128], P(('region', 'within')), as said below
- neighbours: int32 [8192, 5], P(('region', 'within')), may hold values from 0 to 8191, as said below
- tile_counts: int32 [8192], P(('region', 'within')), may hold values from 1 to 5, as said below
- start_block: float32 [1048576, 64], P(('region', 'within'))
Outputs:
- last_block: float32 [1048576, 64], P(('region', 'within'))
- hessenberg: float32 [320, 256], replicated
The draws below stay inside these ranges and needn't reach their ends.
Inputs may be any that keep to these rules, and one draw needn't show every extreme that they name: `neighbours`: slot 0 of every milestone names the milestone itself; the live slots of a milestone name distinct milestones at most 2 away from it; slots that are not live name the milestone itself. `tile_counts`: some milestone has all 5 slots live. `kernel_tiles`: all entries are positive.
All inputs are finite; a program needn't handle non-finite values.
Results may differ from the reference program's by a relative error of at most 0.0075.
Values may be sent and summed in bfloat16 or wider, within the bound.
A program may use at most 64 MiB of HBM per device.

```python
import math
import jax
import jax.numpy as jnp
from jax import lax

STATES = 128
BLOCK = 64
REACH = 2
KMAX = 5
STEPS = 4
M_DEV = 32
NMIL = 8192
NROWS = 1048576


def milestone_graph(key):
    base_key = jax.random.fold_in(key, 7)
    key_score, key_count, key_shift = jax.random.split(base_key, 3)
    milestone = jnp.arange(NMIL, dtype=jnp.int32)
    offset_ids = jnp.arange(2 * REACH, dtype=jnp.int32)
    offsets = jnp.where(offset_ids < REACH, offset_ids - REACH, offset_ids - REACH + 1)
    targets = milestone[:, None] + offsets[None, :]
    valid = (targets >= 0) & (targets < NMIL)
    valid_count = jnp.sum(valid.astype(jnp.int32), axis=1)
    scores = jax.random.randint(key_score, (NMIL, 2 * REACH), 0, 2 ** 20) * (2 * REACH) + offset_ids[None, :]
    scores = scores + jnp.where(valid, 0, 2 ** 26)
    order = jnp.argsort(scores, axis=1, stable=True)
    chosen = jnp.take_along_axis(targets, order, axis=1)[:, :KMAX - 1]
    raw_count = jax.random.randint(key_count, (NMIL,), 1, KMAX + 1)
    shift_value = jax.random.randint(key_shift, (), 0, 29)
    forced = jnp.where(milestone % 29 == shift_value, KMAX, 1)
    counts = jnp.minimum(jnp.maximum(raw_count, forced), valid_count + 1)
    slot_ids = jnp.arange(KMAX, dtype=jnp.int32)
    columns = jnp.concatenate([milestone[:, None], chosen], axis=1)
    columns = jnp.where(slot_ids[None, :] < counts[:, None], columns, milestone[:, None])
    return (columns.astype(jnp.int32), counts.astype(jnp.int32))


def draw_neighbours(key, part):
    columns, counts = milestone_graph(key)
    return columns


def draw_tile_counts(key, part):
    columns, counts = milestone_graph(key)
    return counts


def draw_kernel_tiles(key, part):
    base_key = jax.random.fold_in(key, 11)
    key_base, key_boost = jax.random.split(base_key, 2)
    shape_all = (NMIL, KMAX, STATES, STATES)
    values = jax.random.uniform(key_base, shape_all, jnp.float32, 0.02, 1.0)
    boost = jnp.exp(jax.random.uniform(key_boost, (NMIL, STATES), jnp.float32, 0.0, math.log(8.0)))
    identity = jnp.eye(STATES, dtype=jnp.float32)
    first_slot = (jnp.arange(KMAX) == 0).astype(jnp.float32)
    values = values + first_slot[None, :, None, None] * identity[None, None, :, :] * boost[:, None, :, None]
    return values.astype(jnp.bfloat16)


def draw_start_block(key, part):
    base_key = jax.random.fold_in(key, 13)
    key_value, key_scale = jax.random.split(base_key, 2)
    scales = jnp.exp(jax.random.uniform(key_scale, (NROWS, 1), jnp.float32, 0.0, math.log(10.0)))
    values = jax.random.normal(key_value, (NROWS, BLOCK), jnp.float32)
    return values * scales


def setup_inputs(seed: int = 0) -> dict:
    key_list = jax.random.split(jax.random.key(seed), 5)
    kernel_tiles = draw_kernel_tiles(jax.random.fold_in(key_list[4], 71), 0)
    neighbours = draw_neighbours(jax.random.fold_in(key_list[4], 71), 0)
    tile_counts = draw_tile_counts(jax.random.fold_in(key_list[4], 71), 0)
    start_block = draw_start_block(jax.random.fold_in(key_list[4], 71), 0)
    return {"kernel_tiles": kernel_tiles, "neighbours": neighbours, "tile_counts": tile_counts, "start_block": start_block}


def block_row_sums(kernel_tiles, tile_counts):
    blocks = NMIL // M_DEV

    def one_block(pieces):
        tile_part, count_part = pieces
        live_slots = jnp.arange(KMAX)[None, :] < count_part[:, None]
        masked = jnp.where(live_slots[:, :, None, None], tile_part.astype(jnp.float32), jnp.float32(0.0))
        return jnp.sum(masked, axis=(1, 3))
    summed = lax.map(one_block, (kernel_tiles.reshape(blocks, M_DEV, KMAX, STATES, STATES), tile_counts.reshape(blocks, M_DEV)))
    return summed.reshape(NMIL, STATES)

def apply_kernel(kernel_tiles, neighbours, tile_counts, row_sums, vectors):
    shaped = vectors.astype(jnp.bfloat16).reshape(NMIL, STATES, BLOCK)
    blocks = NMIL // M_DEV

    def one_block(pieces):
        tile_part, column_part, count_part = pieces
        live_slots = jnp.arange(KMAX)[None, :] < count_part[:, None]
        gathered = jnp.where(live_slots[:, :, None, None], shaped[column_part], jnp.zeros((), jnp.bfloat16))
        return jnp.einsum('mkab,mkbc->mac', tile_part.astype(jnp.float32), gathered.astype(jnp.float32))
    result = lax.map(one_block, (kernel_tiles.reshape(blocks, M_DEV, KMAX, STATES, STATES), neighbours.reshape(blocks, M_DEV, KMAX), tile_counts.reshape(blocks, M_DEV)))
    result = result.reshape(NMIL, STATES, BLOCK) / row_sums[:, :, None]
    return result.reshape(NROWS, BLOCK)

def orthonormal(block):
    gram = jnp.dot(block.T, block, precision=lax.Precision.HIGHEST) * (1.0 / NROWS)
    chol_lower = jnp.linalg.cholesky(gram)
    identity = jnp.eye(BLOCK, dtype=block.dtype)
    inverse = jax.scipy.linalg.solve_triangular(chol_lower, identity, lower=True)
    return (jnp.dot(block, inverse.T, precision=lax.Precision.HIGHEST), chol_lower.T)

def reference(kernel_tiles, neighbours, tile_counts, start_block):
    row_sums = block_row_sums(kernel_tiles, tile_counts)
    first_block, unused_factor = orthonormal(start_block)
    krylov_basis = [first_block]
    hessenberg = jnp.zeros(((STEPS + 1) * BLOCK, STEPS * BLOCK), jnp.float32)
    for number in range(STEPS):
        image = apply_kernel(kernel_tiles, neighbours, tile_counts, row_sums, krylov_basis[-1])
        stacked = jnp.concatenate(krylov_basis, axis=1)
        projected = jnp.dot(stacked.T, image, precision=lax.Precision.HIGHEST) * (1.0 / NROWS)
        remainder = image - jnp.dot(stacked, projected, precision=lax.Precision.HIGHEST)
        next_block, factor = orthonormal(remainder)
        hessenberg = hessenberg.at[:(number + 1) * BLOCK, number * BLOCK:(number + 1) * BLOCK].set(projected)
        hessenberg = hessenberg.at[(number + 1) * BLOCK:(number + 2) * BLOCK, number * BLOCK:(number + 1) * BLOCK].set(factor)
        krylov_basis.append(next_block)
    return (krylov_basis[-1], hessenberg)
```

```python
import functools

import jax
import jax.numpy as jnp
from jax import lax
from jax.experimental import pallas as pl
from jax.experimental.pallas import tpu as pltpu
from jax.sharding import PartitionSpec as P

REACH = 2
STEPS = 4
NBLK = STEPS + 1
SHIFTS = (0.0, 0.5, 1.0, 0.25)
F32 = jnp.float32
BF16 = jnp.bfloat16
MESH = pl.DeviceIdType.MESH
HIGHEST = lax.Precision.HIGHEST
NT = (((1,), (1,)), ((), ()))
TN = (((0,), (0,)), ((), ()))
NN = (((1,), (0,)), ((), ()))
ROWS_A, ROWS_B = 384, 256
BATCHES = ((0, ROWS_A), (ROWS_A, ROWS_B))


def place(i, j):
    if j < STEPS:
        t = j * (j + 1) // 2 + i
        return (t // 2) * 64, t % 2
    return ROWS_A + (i // 2) * 64, i % 2


def split(x):
    hi = x.astype(BF16)
    lo = (x - hi.astype(F32)).astype(BF16)
    return jnp.concatenate([hi, lo], axis=0)


def krylov_kernel(
    nr, nw, nbr, cnt, tiles, start, s_out, z_out,
    tl, x0, vb, ones, irs, hb, acc, gb, land1, part, land2, gs,
    in_sem, z_sem, hs, hr, s1, r1, s2, r2, s3, r3,
):
    mil = tl.shape[0]
    slots = tl.shape[1]
    zero_at = mil + 2 * REACH
    n = nr * nw
    me_r = lax.axis_index("region")
    me_w = lax.axis_index("within")
    me = me_r * nw + me_w
    base = me * mil
    right = lax.rem(me + 1, n)
    left = lax.rem(me + n - 1, n)
    right_id = (right // nw, lax.rem(right, nw))
    left_id = (left // nw, lax.rem(left, nw))

    start_copy = pltpu.make_async_copy(start, x0, in_sem.at[0])
    start_copy.start()
    part_mil = mil // 4
    tile_copies = []
    for c in range(4):
        cp = pltpu.make_async_copy(
            tiles.at[pl.ds(c * part_mil, part_mil)],
            tl.at[pl.ds(c * part_mil, part_mil)],
            in_sem.at[1 + c],
        )
        cp.start()
        tile_copies.append(cp)

    barrier = pltpu.get_barrier_semaphore()
    for o in range(1, nr):
        pl.semaphore_signal(
            barrier, inc=1, device_id=(lax.rem(me_r + o, nr), me_w), device_id_type=MESH
        )
    for o in range(1, nw):
        pl.semaphore_signal(
            barrier, inc=1, device_id=(me_r, lax.rem(me_w + o, nw)), device_id_type=MESH
        )
    pl.semaphore_signal(barrier, inc=1, device_id=right_id, device_id_type=MESH)
    pl.semaphore_signal(barrier, inc=1, device_id=left_id, device_id_type=MESH)

    for j in range(STEPS):
        vb[j, zero_at] = jnp.zeros((128, 128), BF16)
    ones[0] = jnp.ones((16, 128), BF16)
    ones[1] = jnp.zeros((16, 128), BF16)
    gb[ROWS_A - 64 : ROWS_A] = jnp.zeros((64, 128), F32)
    gb[ROWS_A + ROWS_B - 64 :] = jnp.zeros((64, 128), F32)

    start_copy.wait()

    def load_start(m):
        lanes = pl.ds(pl.multiple_of(m * 128, 128), 128)
        vb[0, m + REACH] = split(x0[:, lanes])

    edge = list(range(REACH)) + list(range(mil - REACH, mil))
    for m in edge:
        load_start(m)
    pl.semaphore_wait(barrier, nr + nw)

    def halo(j):
        return (
            pltpu.make_async_remote_copy(
                src_ref=vb.at[j, pl.ds(mil, REACH)], dst_ref=hb.at[j, 0],
                send_sem=hs.at[j, 0], recv_sem=hr.at[j, 0],
                device_id=right_id, device_id_type=MESH,
            ),
            pltpu.make_async_remote_copy(
                src_ref=vb.at[j, pl.ds(REACH, REACH)], dst_ref=hb.at[j, 1],
                send_sem=hs.at[j, 1], recv_sem=hr.at[j, 1],
                device_id=left_id, device_id_type=MESH,
            ),
        )

    def start_all(copies):
        for cp in copies:
            cp.start()

    def apply_one(j, m):
        vs, ts = [], []
        for k in range(slots):
            live = k < cnt[m]
            at = jnp.where(live, nbr[k, m] - base + REACH, zero_at)
            v = vb[j, at]
            if j == 0:
                v = jnp.concatenate([v, ones[jnp.where(live, 0, 1)]], axis=0)
            vs.append(v)
            ts.append(tl[m, k])
        prod = lax.dot_general(
            jnp.concatenate(vs, axis=1), jnp.concatenate(ts, axis=1), NT,
            preferred_element_type=F32,
        )
        if j == 0:
            inv = 1.0 / prod[128:136]
            irs[m] = inv
        else:
            inv = irs[m]
        w = (prod[:64] + prod[64:128]) * inv[0:1]
        if SHIFTS[j] != 0.0:
            own = vb[j, m + REACH].astype(F32)
            w = w - SHIFTS[j] * (own[:64] + own[64:])
        vb[j + 1, m + REACH] = split(w)

    group = 8

    def gram(j):
        rows = (j + 1) * 128

        def body(c, carry):
            stack = []
            for i in range(j + 1):
                stack.append(
                    jnp.concatenate(
                        [vb[i, REACH + c * group + q] for q in range(group)], axis=1
                    )
                )
            prod = lax.dot_general(
                jnp.concatenate(stack, axis=0), stack[j], NT, preferred_element_type=F32
            )

            @pl.when(c == 0)
            def _():
                acc[:rows] = prod

            @pl.when(c > 0)
            def _():
                acc[:rows] += prod

            return carry

        lax.fori_loop(0, mil // group, body, 0)
        lane = lax.broadcasted_iota(jnp.int32, (64, 128), 1)
        for i in range(j + 1):
            blk = acc[i * 128 : i * 128 + 64] + acc[i * 128 + 64 : i * 128 + 128]
            blk = blk + pltpu.roll(blk, 64, 1)
            row, odd = place(i, j)
            if odd:
                gb[row : row + 64] = jnp.where(lane < 64, gb[row : row + 64], blk)
            else:
                gb[row : row + 64] = blk

    def rows_of(b, c):
        first, total = BATCHES[b]
        size = total // nr
        return pl.ds(pl.multiple_of(first + c * size, 8), size)

    def stage1(b):
        size = BATCHES[b][1] // nr
        out = []
        for o in range(1, nr):
            to = lax.rem(me_r + o, nr)
            out.append(
                pltpu.make_async_remote_copy(
                    src_ref=gb.at[rows_of(b, to)],
                    dst_ref=land1.at[b, o - 1, pl.ds(0, size)],
                    send_sem=s1.at[b, o - 1], recv_sem=r1.at[b, o - 1],
                    device_id=(to, me_w), device_id_type=MESH,
                )
            )
        return out

    def sum1(b):
        size = BATCHES[b][1] // nr
        total = gb[rows_of(b, me_r)]
        for o in range(1, nr):
            total = total + land1[b, o - 1, 0:size]
        part[b, 0:size] = total
        land2[b, me_w, 0:size] = total

    def stage2(b):
        size = BATCHES[b][1] // nr
        out = []
        for o in range(1, nw):
            to = lax.rem(me_w + o, nw)
            out.append(
                pltpu.make_async_remote_copy(
                    src_ref=part.at[b, pl.ds(0, size)],
                    dst_ref=land2.at[b, me_w, pl.ds(0, size)],
                    send_sem=s2.at[b, o - 1], recv_sem=r2.at[b, o - 1],
                    device_id=(me_r, to), device_id_type=MESH,
                )
            )
        return out

    def wait2(b):
        size = BATCHES[b][1] // nr
        for o in range(1, nw):
            frm = lax.rem(me_w + nw - o, nw)
            pltpu.make_async_remote_copy(
                src_ref=part.at[b, pl.ds(0, size)],
                dst_ref=land2.at[b, frm, pl.ds(0, size)],
                send_sem=s2.at[b, o - 1], recv_sem=r2.at[b, o - 1],
                device_id=(me_r, frm), device_id_type=MESH,
            ).wait_recv()

    def sum2(b):
        size = BATCHES[b][1] // nr
        total = land2[b, 0, 0:size]
        for i in range(1, nw):
            total = total + land2[b, i, 0:size]
        gs[rows_of(b, me_r)] = total

    def stage3(b):
        out = []
        for o in range(1, nr):
            to = lax.rem(me_r + o, nr)
            out.append(
                pltpu.make_async_remote_copy(
                    src_ref=gs.at[rows_of(b, me_r)],
                    dst_ref=gs.at[rows_of(b, me_r)],
                    send_sem=s3.at[b, o - 1], recv_sem=r3.at[b, o - 1],
                    device_id=(to, me_w), device_id_type=MESH,
                )
            )
        return out

    def wait3(b):
        for o in range(1, nr):
            frm = lax.rem(me_r + nr - o, nr)
            pltpu.make_async_remote_copy(
                src_ref=gs.at[rows_of(b, frm)],
                dst_ref=gs.at[rows_of(b, frm)],
                send_sem=s3.at[b, o - 1], recv_sem=r3.at[b, o - 1],
                device_id=(frm, me_w), device_id_type=MESH,
            ).wait_recv()

    def wait_sent(copies):
        for cp in copies:
            cp.wait_send()

    def wait_got(copies):
        for cp in copies:
            cp.wait_recv()

    def interior(fn):
        def body(m, carry):
            fn(m)
            return carry

        lax.fori_loop(REACH, mil - REACH, body, 0, unroll=2)

    halos = [halo(j) for j in range(STEPS)]
    z_copies = [
        pltpu.make_async_copy(vb.at[j, pl.ds(REACH, mil)], z_out.at[j], z_sem.at[j])
        for j in range(NBLK)
    ]
    first = [stage1(b) for b in range(2)]
    second = [stage2(b) for b in range(2)]
    third = [stage3(b) for b in range(2)]

    start_all(halos[0])
    interior(load_start)
    for j in range(STEPS):
        z_copies[j].start()
        gram(j)
        if j == 0:
            for cp in tile_copies:
                cp.wait()
        if j == STEPS - 1:
            start_all(first[0])
        interior(functools.partial(apply_one, j))
        wait_got(halos[j])
        vb[j, 0:REACH] = hb[j, 0]
        vb[j, mil + REACH : mil + 2 * REACH] = hb[j, 1]
        for m in edge:
            apply_one(j, m)
        if j + 1 < STEPS:
            start_all(halos[j + 1])
    z_copies[STEPS].start()
    wait_got(first[0])
    sum1(0)
    start_all(second[0])
    gram(STEPS)
    start_all(first[1])
    wait2(0)
    sum2(0)
    start_all(third[0])
    wait_got(first[1])
    sum1(1)
    start_all(second[1])
    wait3(0)
    wait2(1)
    sum2(1)
    start_all(third[1])
    for j in range(STEPS):
        wait_sent(halos[j])
    for b in range(2):
        wait_sent(first[b])
        wait_sent(second[b])
    wait_sent(third[0])
    for cp in z_copies:
        cp.wait()
    wait3(1)
    s_out[...] = gs[...]
    wait_sent(third[1])


def mm(a, b, dims=NN):
    return lax.dot_general(a, b, dims, precision=HIGHEST, preferred_element_type=F32)


def factor(block):
    size = block.shape[0]
    eye = (
        lax.broadcasted_iota(jnp.int32, (size, size), 0)
        == lax.broadcasted_iota(jnp.int32, (size, size), 1)
    ).astype(F32)
    cur = jnp.concatenate([block, eye], axis=1)
    done = []
    for kb in range(size // 8):
        n = size - 8 * kb
        rid = lax.broadcasted_iota(jnp.int32, (n, 128), 0)
        cols = [
            jnp.broadcast_to(cur[:, 8 * kb + p : 8 * kb + p + 1], (n, 128)) for p in range(8)
        ]
        scale = jnp.zeros((8, 128), F32)
        for p in range(8):
            pivot = cols[p][p : p + 1]
            inv = 1.0 / pivot
            scale = jnp.where(rid[:8] == p, lax.rsqrt(pivot), scale)
            mult = jnp.where(rid > p, cols[p] * inv, 0.0)
            cur = cur - mult * cur[p : p + 1]
            for q in range(p + 1, 8):
                cols[q] = cols[q] - mult * cols[q][p : p + 1]
        done.append(cur[:8] * scale)
        cur = cur[8:]
    full = jnp.concatenate(done, axis=0)
    upper = lax.broadcasted_iota(jnp.int32, (size, size), 0) <= lax.broadcasted_iota(
        jnp.int32, (size, size), 1
    )
    r = jnp.where(upper, full[:, :size], 0.0)
    m = pltpu.roll(full, size, 1)[:, :size]
    return r, m


def finish_kernel(scale, s_ref, z_hbm, q_ref, h_ref, zb, sems):
    mil = zb.shape[1]
    copies = [pltpu.make_async_copy(z_hbm.at[k], zb.at[k], sems.at[k]) for k in range(NBLK)]
    for cp in copies:
        cp.start()

    def gram_block(i, j):
        row, odd = place(i, j)
        x = s_ref[row : row + 64]
        if odd:
            x = pltpu.roll(x, 64, 1)
        return x[:, :64] * scale

    r = [[None] * NBLK for _ in range(NBLK)]
    inv = [[None] * NBLK for _ in range(NBLK)]
    for j in range(NBLK):
        schur = gram_block(j, j)
        if j:
            r_col = None
            for k in range(j):
                stack = jnp.concatenate(
                    [inv[k][i] for i in range(k, j)], axis=0
                )
                term = mm(stack, gram_block(k, j))
                if k:
                    term = jnp.concatenate([jnp.zeros((64 * k, 64), F32), term], axis=0)
                r_col = term if r_col is None else r_col + term
            for i in range(j):
                r[i][j] = r_col[64 * i : 64 * i + 64]
            schur = schur - mm(r_col, r_col, TN)
        r[j][j], inv[j][j] = factor(schur)
        for k in range(j):
            stack = jnp.concatenate([inv[k][i] for i in range(k, j)], axis=0)
            t = mm(r_col[64 * k :], stack, TN)
            inv[k][j] = -mm(inv[j][j], t)

    coef = []
    for k in range(NBLK):
        c = inv[k][STEPS]
        hi = c.astype(BF16)
        lo = (c - hi.astype(F32)).astype(BF16)
        coef.append(
            jnp.concatenate(
                [jnp.concatenate([hi, hi], axis=1), jnp.concatenate([lo, lo], axis=1)], axis=0
            )
        )
    coef = jnp.concatenate(coef, axis=1)

    for j in range(STEPS):
        col = None
        for k in range(j + 1):
            parts = []
            for i in range(k + 2):
                x = r[i][k + 1]
                if i <= k and SHIFTS[k] != 0.0:
                    x = x + SHIFTS[k] * r[i][k]
                parts.append(x)
            term = mm(jnp.concatenate(parts, axis=0), inv[k][j], NT)
            if k < j:
                term = jnp.concatenate([term, jnp.zeros((64 * (j - k), 64), F32)], axis=0)
            col = term if col is None else col + term
        if j + 2 < NBLK:
            col = jnp.concatenate([col, jnp.zeros((64 * (NBLK - j - 2), 64), F32)], axis=0)
        h_ref[:, 64 * j : 64 * j + 64] = col

    for cp in copies:
        cp.wait()

    def body(g, carry):
        m = 2 * g
        right = jnp.concatenate(
            [
                jnp.concatenate([zb[k, m], zb[k, m + 1]], axis=1)
                for k in range(NBLK)
            ],
            axis=0,
        )
        prod = lax.dot_general(coef, right, NN, preferred_element_type=F32)
        q_ref[:, pl.ds(pl.multiple_of(g * 256, 256), 256)] = prod[:64] + prod[64:]
        return carry

    lax.fori_loop(0, mil // 2, body, 0)


def on_device(nr, nw, kernel_tiles, neighbours, tile_counts, start_block):
    mil, slots, states = kernel_tiles.shape[:3]
    width = start_block.shape[1]
    rows = mil * states
    vmem = pl.BlockSpec(memory_space=pltpu.VMEM)
    smem = pl.BlockSpec(memory_space=pltpu.SMEM)
    hbm = pl.BlockSpec(memory_space=pl.ANY)
    size = ROWS_A // nr
    dma = pltpu.SemaphoreType.DMA
    packed, z = pl.pallas_call(
        functools.partial(krylov_kernel, nr, nw),
        out_shape=(
            jax.ShapeDtypeStruct((ROWS_A + ROWS_B, 128), F32),
            jax.ShapeDtypeStruct((NBLK, mil, 2 * width, states), BF16),
        ),
        in_specs=[smem, smem, hbm, hbm],
        out_specs=(vmem, hbm),
        scratch_shapes=[
            pltpu.VMEM((mil, slots, states, states), BF16),
            pltpu.VMEM((width, rows), F32),
            pltpu.VMEM((NBLK, mil + 2 * REACH + 1, 2 * width, states), BF16),
            pltpu.VMEM((2, 16, 128), BF16),
            pltpu.VMEM((mil, 8, 128), F32),
            pltpu.VMEM((STEPS, 2, REACH, 2 * width, states), BF16),
            pltpu.VMEM((NBLK * 128, 128), F32),
            pltpu.VMEM((ROWS_A + ROWS_B, 128), F32),
            pltpu.VMEM((2, nr, size, 128), F32),
            pltpu.VMEM((2, size, 128), F32),
            pltpu.VMEM((2, nw, size, 128), F32),
            pltpu.VMEM((ROWS_A + ROWS_B, 128), F32),
            dma((5,)), dma((NBLK,)),
            dma((STEPS, 2)), dma((STEPS, 2)),
            dma((2, nr)), dma((2, nr)),
            dma((2, nw)), dma((2, nw)),
            dma((2, nr)), dma((2, nr)),
        ],
        compiler_params=pltpu.CompilerParams(
            collective_id=0, has_side_effects=True, vmem_limit_bytes=40 * 1024 * 1024
        ),
    )(neighbours.T, tile_counts, kernel_tiles, start_block.T)
    last, hess = pl.pallas_call(
        functools.partial(finish_kernel, 1.0 / (rows * nr * nw)),
        out_shape=(
            jax.ShapeDtypeStruct((width, rows), F32),
            jax.ShapeDtypeStruct((NBLK * width, STEPS * width), F32),
        ),
        in_specs=[vmem, hbm],
        out_specs=(vmem, vmem),
        scratch_shapes=[
            pltpu.VMEM((NBLK, mil, 2 * width, states), BF16),
            dma((NBLK,)),
        ],
        compiler_params=pltpu.CompilerParams(vmem_limit_bytes=40 * 1024 * 1024),
    )(packed, z)
    return last.T, hess


def solution(mesh):
    nr, nw = mesh.shape["region"], mesh.shape["within"]
    return jax.shard_map(
        functools.partial(on_device, nr, nw),
        mesh=mesh,
        in_specs=(
            P(("region", "within"), None, None, None),
            P(("region", "within"), None),
            P(("region", "within")),
            P(("region", "within"), None),
        ),
        out_specs=(P(("region", "within"), None), P()),
        check_vma=False,
    )
```

```python
import functools

import jax
import jax.numpy as jnp
from jax import lax
from jax.experimental import pallas as pl
from jax.experimental.pallas import tpu as pltpu
from jax.sharding import PartitionSpec as P

REACH = 2
STEPS = 4
NBLK = STEPS + 1
SHIFTS = (0.0, 0.5, 1.0, 0.25)
F32 = jnp.float32
BF16 = jnp.bfloat16
MESH = pl.DeviceIdType.MESH
HIGHEST = lax.Precision.HIGHEST
NT = (((1,), (1,)), ((), ()))
TN = (((0,), (0,)), ((), ()))
NN = (((1,), (0,)), ((), ()))
BATCHES = ((0, 256), (256, 128), (384, 256))
GRAM_ROWS = 640


def batch_of(j):
    return max(j - 2, 0)


def place(i, j):
    t = j * (j + 1) // 2 + i if j < 3 else i
    return BATCHES[batch_of(j)][0] + (t // 2) * 64, t % 2


def split(x):
    hi = x.astype(BF16)
    lo = (x - hi.astype(F32)).astype(BF16)
    return jnp.concatenate([hi, lo], axis=0)


def mm(a, b, dims=NN):
    return lax.dot_general(a, b, dims, precision=HIGHEST, preferred_element_type=F32)


def gram_block(ref, scale, i, j, first=0):
    row, odd = place(i, j)
    x = ref[row - first : row - first + 64]
    if odd:
        x = pltpu.roll(x, 64, 1)
    return x[:, :64] * scale


def factor(block):
    size = block.shape[0]
    eye = (
        lax.broadcasted_iota(jnp.int32, (size, size), 0)
        == lax.broadcasted_iota(jnp.int32, (size, size), 1)
    ).astype(F32)
    cur = jnp.concatenate([block, eye], axis=1)
    done = []
    for kb in range(size // 8):
        n = size - 8 * kb
        rid = lax.broadcasted_iota(jnp.int32, (n, 128), 0)
        cols = [
            jnp.broadcast_to(cur[:, 8 * kb + p : 8 * kb + p + 1], (n, 128)) for p in range(8)
        ]
        scale = jnp.zeros((8, 128), F32)
        for p in range(8):
            pivot = cols[p][p : p + 1]
            inv = 1.0 / pivot
            scale = jnp.where(rid[:8] == p, lax.rsqrt(pivot), scale)
            mult = jnp.where(rid > p, cols[p] * inv, 0.0)
            cur = cur - mult * cur[p : p + 1]
            for q in range(p + 1, 8):
                cols[q] = cols[q] - mult * cols[q][p : p + 1]
        done.append(cur[:8] * scale)
        cur = cur[8:]
    full = jnp.concatenate(done, axis=0)
    upper = lax.broadcasted_iota(jnp.int32, (size, size), 0) <= lax.broadcasted_iota(
        jnp.int32, (size, size), 1
    )
    r = jnp.where(upper, full[:, :size], 0.0)
    m = pltpu.roll(full, size, 1)[:, :size]
    return r, m


def krylov_kernel(
    nr, nw, scale, nbr_hbm, cnt_hbm, tiles, start, s_out, inv_out, h_out, z_out,
    nbr, cnt, tl, x0, v0, v1, v2, v3, v4, ones, irs, hb, acc, gb, land1, part, land2, gs, bm,
    in_sem, z_sem, hs, hr, s1, r1, s2, r2, s3, r3,
):
    vb = (v0, v1, v2, v3, v4)
    mil = tl.shape[0]
    slots = tl.shape[1]
    zero_at = mil + 2 * REACH
    n = nr * nw
    me_r = lax.axis_index("region")
    me_w = lax.axis_index("within")
    me = me_r * nw + me_w
    base = me * mil
    right = lax.rem(me + 1, n)
    left = lax.rem(me + n - 1, n)
    right_id = (right // nw, lax.rem(right, nw))
    left_id = (left // nw, lax.rem(left, nw))

    start_copy = pltpu.make_async_copy(start, x0, in_sem.at[0])
    start_copy.start()
    index_copies = (
        pltpu.make_async_copy(nbr_hbm, nbr, in_sem.at[5]),
        pltpu.make_async_copy(cnt_hbm, cnt, in_sem.at[6]),
    )
    for cp in index_copies:
        cp.start()
    part_mil = mil // 4
    tile_copies = []
    for c in range(4):
        cp = pltpu.make_async_copy(
            tiles.at[pl.ds(c * part_mil, part_mil)],
            tl.at[pl.ds(c * part_mil, part_mil)],
            in_sem.at[1 + c],
        )
        cp.start()
        tile_copies.append(cp)

    barrier = pltpu.get_barrier_semaphore()
    for o in range(1, nr):
        pl.semaphore_signal(
            barrier, inc=1, device_id=(lax.rem(me_r + o, nr), me_w), device_id_type=MESH
        )
    for o in range(1, nw):
        pl.semaphore_signal(
            barrier, inc=1, device_id=(me_r, lax.rem(me_w + o, nw)), device_id_type=MESH
        )
    pl.semaphore_signal(barrier, inc=1, device_id=right_id, device_id_type=MESH)
    pl.semaphore_signal(barrier, inc=1, device_id=left_id, device_id_type=MESH)

    for j in range(STEPS):
        vb[j][zero_at] = jnp.zeros((128, 128), BF16)
    ones[0] = jnp.ones((16, 128), BF16)
    ones[1] = jnp.zeros((16, 128), BF16)
    for b in (0, 2):
        first, total = BATCHES[b]
        gb[first + total - 64 : first + total] = jnp.zeros((64, 128), F32)
    inv_out[...] = jnp.zeros(inv_out.shape, F32)
    bm[...] = jnp.zeros(bm.shape, F32)

    start_copy.wait()

    def load_start(m):
        lanes = pl.ds(pl.multiple_of(m * 128, 128), 128)
        vb[0][m + REACH] = split(x0[:, lanes])

    edge = list(range(REACH)) + list(range(mil - REACH, mil))
    for m in edge:
        load_start(m)
    pl.semaphore_wait(barrier, nr + nw)

    def halo(j):
        return (
            pltpu.make_async_remote_copy(
                src_ref=vb[j].at[pl.ds(mil, REACH)], dst_ref=hb.at[j, 0],
                send_sem=hs.at[j, 0], recv_sem=hr.at[j, 0],
                device_id=right_id, device_id_type=MESH,
            ),
            pltpu.make_async_remote_copy(
                src_ref=vb[j].at[pl.ds(REACH, REACH)], dst_ref=hb.at[j, 1],
                send_sem=hs.at[j, 1], recv_sem=hr.at[j, 1],
                device_id=left_id, device_id_type=MESH,
            ),
        )

    def start_all(copies):
        for cp in copies:
            cp.start()

    def apply_one(j, m):
        vs, ts = [], []
        for k in range(slots):
            live = k < cnt[m]
            at = jnp.where(live, nbr[k, m] - base + REACH, zero_at)
            v = vb[j][at]
            if j == 0:
                v = jnp.concatenate([v, ones[jnp.where(live, 0, 1)]], axis=0)
            vs.append(v)
            ts.append(tl[m, k])
        prod = lax.dot_general(
            jnp.concatenate(vs, axis=1), jnp.concatenate(ts, axis=1), NT,
            preferred_element_type=F32,
        )
        if j == 0:
            inv = 1.0 / prod[128:136]
            irs[m] = inv
        else:
            inv = irs[m]
        w = (prod[:64] + prod[64:128]) * inv[0:1]
        if SHIFTS[j] != 0.0:
            own = vb[j][m + REACH].astype(F32)
            w = w - SHIFTS[j] * (own[:64] + own[64:])
        vb[j + 1][m + REACH] = split(w)

    group = mil // 2

    def gram(j):
        rows = (j + 1) * 128
        for c in range(mil // group):
            stack = [
                jnp.concatenate([vb[i][REACH + c * group + q] for q in range(group)], axis=1)
                for i in range(j + 1)
            ]
            prod = lax.dot_general(
                jnp.concatenate(stack, axis=0), stack[j], NT, preferred_element_type=F32
            )
            if c == 0:
                acc[:rows] = prod
            else:
                acc[:rows] += prod
        lane = lax.broadcasted_iota(jnp.int32, (64, 128), 1)
        for i in range(j + 1):
            blk = acc[i * 128 : i * 128 + 64] + acc[i * 128 + 64 : i * 128 + 128]
            blk = blk + pltpu.roll(blk, 64, 1)
            row, odd = place(i, j)
            if odd:
                gb[row : row + 64] = jnp.where(lane < 64, gb[row : row + 64], blk)
            else:
                gb[row : row + 64] = blk

    def rows_of(b, c):
        first, total = BATCHES[b]
        size = total // nr
        return pl.ds(pl.multiple_of(first + c * size, 8), size)

    def stage1(b):
        size = BATCHES[b][1] // nr
        out = []
        for o in range(1, nr):
            to = lax.rem(me_r + o, nr)
            out.append(
                pltpu.make_async_remote_copy(
                    src_ref=gb.at[rows_of(b, to)],
                    dst_ref=land1.at[b, o - 1, pl.ds(0, size)],
                    send_sem=s1.at[b, o - 1], recv_sem=r1.at[b, o - 1],
                    device_id=(to, me_w), device_id_type=MESH,
                )
            )
        return out

    def sum1(b):
        size = BATCHES[b][1] // nr
        total = gb[rows_of(b, me_r)]
        for o in range(1, nr):
            total = total + land1[b, o - 1, 0:size]
        part[b, 0:size] = total
        land2[b, me_w, 0:size] = total

    def stage2(b):
        size = BATCHES[b][1] // nr
        out = []
        for o in range(1, nw):
            to = lax.rem(me_w + o, nw)
            out.append(
                pltpu.make_async_remote_copy(
                    src_ref=part.at[b, pl.ds(0, size)],
                    dst_ref=land2.at[b, me_w, pl.ds(0, size)],
                    send_sem=s2.at[b, o - 1], recv_sem=r2.at[b, o - 1],
                    device_id=(me_r, to), device_id_type=MESH,
                )
            )
        return out

    def wait2(b):
        size = BATCHES[b][1] // nr
        for o in range(1, nw):
            frm = lax.rem(me_w + nw - o, nw)
            pltpu.make_async_remote_copy(
                src_ref=part.at[b, pl.ds(0, size)],
                dst_ref=land2.at[b, frm, pl.ds(0, size)],
                send_sem=s2.at[b, o - 1], recv_sem=r2.at[b, o - 1],
                device_id=(me_r, frm), device_id_type=MESH,
            ).wait_recv()

    def sum2(b):
        size = BATCHES[b][1] // nr
        total = land2[b, 0, 0:size]
        for i in range(1, nw):
            total = total + land2[b, i, 0:size]
        gs[rows_of(b, me_r)] = total

    def stage3(b):
        out = []
        for o in range(1, nr):
            to = lax.rem(me_r + o, nr)
            out.append(
                pltpu.make_async_remote_copy(
                    src_ref=gs.at[rows_of(b, me_r)],
                    dst_ref=gs.at[rows_of(b, me_r)],
                    send_sem=s3.at[b, o - 1], recv_sem=r3.at[b, o - 1],
                    device_id=(to, me_w), device_id_type=MESH,
                )
            )
        return out

    def wait3(b):
        for o in range(1, nr):
            frm = lax.rem(me_r + nr - o, nr)
            pltpu.make_async_remote_copy(
                src_ref=gs.at[rows_of(b, frm)],
                dst_ref=gs.at[rows_of(b, frm)],
                send_sem=s3.at[b, o - 1], recv_sem=r3.at[b, o - 1],
                device_id=(frm, me_w), device_id_type=MESH,
            ).wait_recv()

    def wait_sent(copies):
        for cp in copies:
            cp.wait_send()

    def wait_got(copies):
        for cp in copies:
            cp.wait_recv()

    def interior(fn, lo=REACH, hi=mil - REACH):
        def body(m, carry):
            fn(m)
            return carry

        lax.fori_loop(lo, hi, body, 0, unroll=14)

    def chain(j):
        n = 64 * j
        blocks = [gram_block(gs, scale, i, j) for i in range(j + 1)]
        schur = blocks[j]
        if j:
            known = inv_out[0:n, 0:n]
            above = mm(known, jnp.concatenate(blocks[:j], axis=0))
            schur = schur - mm(above, above, TN)
        r, m = factor(schur)
        col = r
        if j:
            inv_out[n : n + 64, 0:n] = -mm(m, mm(above, known, TN))
            col = jnp.concatenate([above, r], axis=0)
            bm[0 : n + 64, n - 64 : n] += col
        inv_out[n : n + 64, n : n + 64] = m
        bm[0 : n + 64, n : n + 64] = SHIFTS[j] * col

    halos = [halo(j) for j in range(STEPS)]
    z_copies = [
        pltpu.make_async_copy(vb[j].at[pl.ds(REACH, mil)], z_out.at[j], z_sem.at[j])
        for j in range(NBLK)
    ]
    first = [stage1(b) for b in range(3)]
    second = [stage2(b) for b in range(3)]
    third = [stage3(b) for b in range(3)]

    def forward1(b):
        wait_got(first[b])
        sum1(b)
        start_all(second[b])

    def forward2(b):
        wait2(b)
        sum2(b)
        start_all(third[b])

    start_all(halos[0])
    interior(load_start)
    middle = mil // 2
    for j in range(STEPS):
        z_copies[j].start()
        gram(j)
        if j == 0:
            for cp in tile_copies:
                cp.wait()
            for cp in index_copies:
                cp.wait()
        step = functools.partial(apply_one, j)
        if j >= 2:
            start_all(first[j - 2])
        if j == STEPS - 1:
            interior(step, REACH, middle)
            forward1(0)
            interior(step, middle, mil - REACH)
        else:
            interior(step)
        wait_got(halos[j])
        vb[j][0:REACH] = hb[j, 0]
        vb[j][mil + REACH : mil + 2 * REACH] = hb[j, 1]
        for m in edge:
            apply_one(j, m)
        if j + 1 < STEPS:
            start_all(halos[j + 1])
    z_copies[STEPS].start()
    gram(STEPS)
    start_all(first[2])
    forward1(1)
    forward2(0)
    for j in range(STEPS):
        wait_sent(halos[j])
    forward1(2)
    forward2(1)
    wait3(0)
    chain(0)
    chain(1)
    forward2(2)
    chain(2)
    wait3(1)
    chain(3)
    h_out[...] = mm(bm[...], inv_out[...], NT)
    for b in range(3):
        wait_sent(first[b])
        wait_sent(second[b])
    wait_sent(third[0])
    wait_sent(third[1])
    for cp in z_copies:
        cp.wait()
    wait3(2)
    s_out[...] = gs[BATCHES[2][0] :]
    wait_sent(third[2])


def finish_kernel(scale, s_ref, inv_ref, hp_ref, z_hbm, q_ref, h_ref, zb, sems):
    mil = zb.shape[1]
    copies = [pltpu.make_async_copy(z_hbm.at[k], zb.at[k], sems.at[k]) for k in range(NBLK)]
    for cp in copies:
        cp.start()

    n = 64 * STEPS
    blocks = [gram_block(s_ref, scale, i, STEPS, BATCHES[2][0]) for i in range(NBLK)]
    known = inv_ref[...]
    above = mm(known, jnp.concatenate(blocks[:STEPS], axis=0))
    r, m = factor(blocks[STEPS] - mm(above, above, TN))
    row = -mm(m, mm(above, known, TN))
    coef = []
    for k in range(NBLK):
        c = m
        if k < STEPS:
            c = row[:, 128 * (k // 2) : 128 * (k // 2) + 128]
            if k % 2:
                c = pltpu.roll(c, 64, 1)
            c = c[:, :64]
        hi = c.astype(BF16)
        lo = (c - hi.astype(F32)).astype(BF16)
        coef.append(
            jnp.concatenate(
                [jnp.concatenate([hi, hi], axis=1), jnp.concatenate([lo, lo], axis=1)], axis=0
            )
        )
    coef = jnp.concatenate(coef, axis=1)

    corner = pltpu.roll(inv_ref[n - 64 : n, n - 128 : n], 64, 1)[:, :64]
    h_ref[:, 0 : n - 64] = hp_ref[:, 0 : n - 64]
    h_ref[:, n - 64 : n] = hp_ref[:, n - 64 : n] + mm(
        jnp.concatenate([above, r], axis=0), corner, NT
    )

    for cp in copies:
        cp.wait()

    def body(g, carry):
        right = jnp.concatenate(
            [jnp.concatenate([zb[k, 2 * g], zb[k, 2 * g + 1]], axis=1) for k in range(NBLK)],
            axis=0,
        )
        prod = lax.dot_general(coef, right, NN, preferred_element_type=F32)
        q_ref[:, pl.ds(pl.multiple_of(g * 256, 256), 256)] = prod[:64] + prod[64:]
        return carry

    lax.fori_loop(0, mil // 2, body, 0, unroll=8)


def in_hbm(*arrays):
    return [pltpu.with_memory_space_constraint(a, pltpu.HBM) for a in arrays]


def on_device(nr, nw, kernel_tiles, neighbours, tile_counts, start_block):
    mil, slots, states = kernel_tiles.shape[:3]
    width = start_block.shape[1]
    rows = mil * states
    scale = 1.0 / (rows * nr * nw)
    vmem = pl.BlockSpec(memory_space=pltpu.VMEM)
    hbm = pl.BlockSpec(memory_space=pltpu.HBM)
    size = 256 // nr
    square = STEPS * width
    dma = pltpu.SemaphoreType.DMA
    vec = pltpu.VMEM((mil + 2 * REACH + 1, 2 * width, states), BF16)
    packed, inv, part, z = pl.pallas_call(
        functools.partial(krylov_kernel, nr, nw, scale),
        out_shape=(
            jax.ShapeDtypeStruct((256, 128), F32),
            jax.ShapeDtypeStruct((square, square), F32),
            jax.ShapeDtypeStruct((NBLK * width, square), F32),
            jax.ShapeDtypeStruct((NBLK, mil, 2 * width, states), BF16),
        ),
        in_specs=[hbm, hbm, hbm, hbm],
        out_specs=(vmem, vmem, vmem, hbm),
        scratch_shapes=[
            pltpu.SMEM((slots, mil), jnp.int32),
            pltpu.SMEM((mil,), jnp.int32),
            pltpu.VMEM((mil, slots, states, states), BF16),
            pltpu.VMEM((width, rows), F32),
            vec, vec, vec, vec, vec,
            pltpu.VMEM((2, 16, 128), BF16),
            pltpu.VMEM((mil, 8, 128), F32),
            pltpu.VMEM((STEPS, 2, REACH, 2 * width, states), BF16),
            pltpu.VMEM((NBLK * 128, 128), F32),
            pltpu.VMEM((GRAM_ROWS, 128), F32),
            pltpu.VMEM((3, nr, size, 128), F32),
            pltpu.VMEM((3, size, 128), F32),
            pltpu.VMEM((3, nw, size, 128), F32),
            pltpu.VMEM((GRAM_ROWS, 128), F32),
            pltpu.VMEM((NBLK * width, square), F32),
            dma((7,)), dma((NBLK,)),
            dma((STEPS, 2)), dma((STEPS, 2)),
            dma((3, nr)), dma((3, nr)),
            dma((3, nw)), dma((3, nw)),
            dma((3, nr)), dma((3, nr)),
        ],
        compiler_params=pltpu.CompilerParams(
            collective_id=0, has_side_effects=True, vmem_limit_bytes=40 * 1024 * 1024
        ),
    )(*in_hbm(neighbours.T, tile_counts, kernel_tiles, start_block.T))
    last, hess = pl.pallas_call(
        functools.partial(finish_kernel, scale),
        out_shape=(
            jax.ShapeDtypeStruct((width, rows), F32),
            jax.ShapeDtypeStruct((NBLK * width, square), F32),
        ),
        in_specs=[vmem, vmem, vmem, hbm],
        out_specs=(vmem, vmem),
        scratch_shapes=[
            pltpu.VMEM((NBLK, mil, 2 * width, states), BF16),
            dma((NBLK,)),
        ],
        compiler_params=pltpu.CompilerParams(vmem_limit_bytes=40 * 1024 * 1024),
    )(packed, inv, part, z)
    return last.T, hess


def solution(mesh):
    nr, nw = mesh.shape["region"], mesh.shape["within"]
    return jax.shard_map(
        functools.partial(on_device, nr, nw),
        mesh=mesh,
        in_specs=(
            P(("region", "within"), None, None, None),
            P(("region", "within"), None),
            P(("region", "within")),
            P(("region", "within"), None),
        ),
        out_specs=(P(("region", "within"), None), P()),
        check_vma=False,
    )
```

```python
import functools

import jax
import jax.numpy as jnp
from jax import lax
from jax.experimental import pallas as pl
from jax.experimental.pallas import tpu as pltpu
from jax.sharding import PartitionSpec as P

REACH = 2
STEPS = 4
NBLK = STEPS + 1
SHIFTS = (0.0, 0.5, 1.0, 0.25)
F32 = jnp.float32
BF16 = jnp.bfloat16
MESH = pl.DeviceIdType.MESH
HIGHEST = lax.Precision.HIGHEST
NT = (((1,), (1,)), ((), ()))
TN = (((0,), (0,)), ((), ()))
NN = (((1,), (0,)), ((), ()))
BATCHES = ((0, 256), (256, 128), (384, 256))
GRAM_ROWS = 640

def place(i, j):
    t = i + (j * (j + 1) // 2 if j < 3 else 0)
    return BATCHES[max(j - 2, 0)][0] + (t // 2) * 64, t % 2


def split(x):
    hi = x.astype(BF16)
    lo = (x - hi.astype(F32)).astype(BF16)
    return jnp.concatenate([hi, lo], axis=0)


def mm(a, b, dims=NN):
    return lax.dot_general(a, b, dims, precision=HIGHEST, preferred_element_type=F32)


def gram_block(ref, scale, i, j, first=0):
    row, odd = place(i, j)
    x = ref[row - first : row - first + 64]
    if odd:
        x = pltpu.roll(x, 64, 1)
    return x[:, :64] * scale


def factor(block):
    size = block.shape[0]
    eye = (
        lax.broadcasted_iota(jnp.int32, (size, size), 0)
        == lax.broadcasted_iota(jnp.int32, (size, size), 1)
    ).astype(F32)
    cur = jnp.concatenate([block, eye], axis=1)
    done = []
    for kb in range(size // 8):
        n = size - 8 * kb
        rid = lax.broadcasted_iota(jnp.int32, (n, 128), 0)
        cols = [
            jnp.broadcast_to(cur[:, 8 * kb + p : 8 * kb + p + 1], (n, 128)) for p in range(8)
        ]
        scale = jnp.zeros((8, 128), F32)
        for p in range(0, 8, 2):
            a, b, c = cols[p][p : p + 1], cols[p][p + 1 : p + 2], cols[p + 1][p + 1 : p + 2]
            det = a * c - b * b
            inv_a = 1.0 / a
            inv_c = a * (1.0 / det)
            ratio = b * inv_a
            scale = jnp.where(rid[:8] == p, lax.rsqrt(a), scale)
            scale = jnp.where(rid[:8] == p + 1, lax.rsqrt(det * inv_a), scale)
            mult0 = jnp.where(rid > p, cols[p] * inv_a, 0.0)
            mult1 = jnp.where(rid > p + 1, (cols[p + 1] - mult0 * b) * inv_c, 0.0)
            row0 = cur[p : p + 1]
            row1 = cur[p + 1 : p + 2] - ratio * row0
            cur = cur - mult0 * row0 - mult1 * row1
            for q in range(p + 2, 8):
                q0 = cols[q][p : p + 1]
                q1 = cols[q][p + 1 : p + 2] - ratio * q0
                cols[q] = cols[q] - mult0 * q0 - mult1 * q1
        done.append(cur[:8] * scale)
        cur = cur[8:]
    full = jnp.concatenate(done, axis=0)
    upper = lax.broadcasted_iota(jnp.int32, (size, size), 0) <= lax.broadcasted_iota(
        jnp.int32, (size, size), 1
    )
    r = jnp.where(upper, full[:, :size], 0.0)
    m = pltpu.roll(full, size, 1)[:, :size]
    return r, m


def krylov_kernel(
    nr, nw, scale, nbr_hbm, cnt_hbm, tiles, start, s_out, inv_out, bm, z_out,
    nbr, cnt, tl, x0, v0, v1, v2, v3, v4, ones, irs, hb, acc, gb, land1, part, land2, gs,
    in_sem, z_sem, hs, hr, s1, r1, s2, r2, s3, r3,
):
    vb = (v0, v1, v2, v3, v4)
    mil = z_out.shape[1]
    slots = tl.shape[1]
    zero_at = mil + 2 * REACH
    n = nr * nw
    me_r = lax.axis_index("region")
    me_w = lax.axis_index("within")
    me = me_r * nw + me_w
    base = me * mil
    right = lax.rem(me + 1, n)
    left = lax.rem(me + n - 1, n)
    right_id = (right // nw, lax.rem(right, nw))
    left_id = (left // nw, lax.rem(left, nw))

    barrier = pltpu.get_barrier_semaphore()
    for o in range(1, nr):
        pl.semaphore_signal(
            barrier, inc=1, device_id=(lax.rem(me_r + o, nr), me_w), device_id_type=MESH
        )
    for o in range(1, nw):
        pl.semaphore_signal(
            barrier, inc=1, device_id=(me_r, lax.rem(me_w + o, nw)), device_id_type=MESH
        )
    pl.semaphore_signal(barrier, inc=1, device_id=right_id, device_id_type=MESH)
    pl.semaphore_signal(barrier, inc=1, device_id=left_id, device_id_type=MESH)

    start_copy = pltpu.make_async_copy(start, x0, in_sem.at[0])
    start_copy.start()
    index_copies = (
        pltpu.make_async_copy(nbr_hbm, nbr, in_sem.at[5]),
        pltpu.make_async_copy(cnt_hbm, cnt, in_sem.at[6]),
    )
    for cp in index_copies:
        cp.start()
    part_mil = mil // 4
    tile_copies = []
    for c in range(4):
        cp = pltpu.make_async_copy(
            tiles.at[pl.ds(c * part_mil, part_mil)],
            tl.at[pl.ds(c * part_mil, part_mil)],
            in_sem.at[1 + c],
        )
        cp.start()
        tile_copies.append(cp)

    for j in range(STEPS):
        vb[j][zero_at] = jnp.zeros((128, 128), BF16)
    ones[0] = jnp.ones((16, 128), BF16)
    ones[1] = jnp.zeros((16, 128), BF16)
    for row in (192, GRAM_ROWS - 64):
        gb[row : row + 64] = jnp.zeros((64, 128), F32)
    inv_out[...] = jnp.zeros(inv_out.shape, F32)
    bm[...] = jnp.zeros(bm.shape, F32)

    start_copy.wait()

    def load_start(m):
        lanes = pl.ds(pl.multiple_of(m * 128, 128), 128)
        vb[0][m + REACH] = split(x0[:, lanes])

    for m in list(range(REACH)) + list(range(mil - REACH, mil)):
        load_start(m)
    pl.semaphore_wait(barrier, nr + nw)

    def halo(j):
        return (
            pltpu.make_async_remote_copy(
                src_ref=vb[j].at[pl.ds(mil, REACH)], dst_ref=hb.at[j, 0],
                send_sem=hs.at[j, 0], recv_sem=hr.at[j, 0],
                device_id=right_id, device_id_type=MESH,
            ),
            pltpu.make_async_remote_copy(
                src_ref=vb[j].at[pl.ds(REACH, REACH)], dst_ref=hb.at[j, 1],
                send_sem=hs.at[j, 1], recv_sem=hr.at[j, 1],
                device_id=left_id, device_id_type=MESH,
            ),
        )

    def start_all(copies):
        for cp in copies:
            cp.start()

    def apply_one(j, m):
        vs, tiles_m = [], []
        for k in range(slots):
            live = k < cnt[m]
            at = jnp.where(live, nbr[k, m] - base + REACH, zero_at)
            v = vb[j][at]
            if j == 0:
                v = jnp.concatenate([v, ones[jnp.where(live, 0, 1)]], axis=0)
            vs.append(v)
            tiles_m.append(tl[m, k])
        prod = lax.dot_general(
            jnp.concatenate(vs, axis=1), jnp.concatenate(tiles_m, axis=1), NT,
            preferred_element_type=F32,
        )
        if j == 0:
            inv = 1.0 / prod[128:136]
            irs[m] = inv
        else:
            inv = irs[m]
        w = (prod[:64] + prod[64:128]) * inv[0:1]
        if SHIFTS[j] != 0.0:
            own = vb[j][m + REACH].astype(F32)
            w = w - SHIFTS[j] * (own[:64] + own[64:])
        vb[j + 1][m + REACH] = split(w)

    def accumulate(j, milestones, fresh):
        rows = (j + 1) * 128
        stack = [
            jnp.concatenate([vb[i][REACH + m] for m in milestones], axis=1) for i in range(j + 1)
        ]
        prod = lax.dot_general(
            jnp.concatenate(stack, axis=0), stack[j], NT, preferred_element_type=F32
        )
        if fresh:
            acc[:rows] = prod
        else:
            acc[:rows] += prod

    def gram(j):
        accumulate(j, range(mil // 2), True)
        accumulate(j, range(mil // 2, mil), False)
        fold(j)

    def fold(j):
        lane = lax.broadcasted_iota(jnp.int32, (64, 128), 1)
        for i in range(j + 1):
            blk = acc[i * 128 : i * 128 + 64] + acc[i * 128 + 64 : i * 128 + 128]
            blk = blk + pltpu.roll(blk, 64, 1)
            row, odd = place(i, j)
            if odd:
                gb[row : row + 64] = jnp.where(lane < 64, gb[row : row + 64], blk)
            else:
                gb[row : row + 64] = blk

    def rows_of(b, c):
        first, total = BATCHES[b]
        size = total // nr
        return pl.ds(pl.multiple_of(first + c * size, 8), size)

    def stage1(b):
        size = BATCHES[b][1] // nr
        out = []
        for o in range(1, nr):
            to = lax.rem(me_r + o, nr)
            out.append(
                pltpu.make_async_remote_copy(
                    src_ref=gb.at[rows_of(b, to)],
                    dst_ref=land1.at[b, o - 1, pl.ds(0, size)],
                    send_sem=s1.at[b, o - 1], recv_sem=r1.at[b, o - 1],
                    device_id=(to, me_w), device_id_type=MESH,
                )
            )
        return out

    def sum1(b):
        size = BATCHES[b][1] // nr
        total = gb[rows_of(b, me_r)]
        for o in range(1, nr):
            total = total + land1[b, o - 1, 0:size]
        part[b, 0:size] = total
        land2[b, me_w, 0:size] = total

    def stage2(b):
        size = BATCHES[b][1] // nr
        out = []
        for o in range(1, nw):
            to = lax.rem(me_w + o, nw)
            out.append(
                pltpu.make_async_remote_copy(
                    src_ref=part.at[b, pl.ds(0, size)],
                    dst_ref=land2.at[b, me_w, pl.ds(0, size)],
                    send_sem=s2.at[b, o - 1], recv_sem=r2.at[b, o - 1],
                    device_id=(me_r, to), device_id_type=MESH,
                )
            )
        return out

    def wait2(b):
        size = BATCHES[b][1] // nr
        for o in range(1, nw):
            frm = lax.rem(me_w + nw - o, nw)
            pltpu.make_async_remote_copy(
                src_ref=part.at[b, pl.ds(0, size)],
                dst_ref=land2.at[b, frm, pl.ds(0, size)],
                send_sem=s2.at[b, o - 1], recv_sem=r2.at[b, o - 1],
                device_id=(me_r, frm), device_id_type=MESH,
            ).wait_recv()

    def sum2(b):
        size = BATCHES[b][1] // nr
        total = land2[b, 0, 0:size]
        for i in range(1, nw):
            total = total + land2[b, i, 0:size]
        gs[rows_of(b, me_r)] = total

    def stage3(b):
        out = []
        for o in range(1, nr):
            to = lax.rem(me_r + o, nr)
            out.append(
                pltpu.make_async_remote_copy(
                    src_ref=gs.at[rows_of(b, me_r)],
                    dst_ref=gs.at[rows_of(b, me_r)],
                    send_sem=s3.at[b, o - 1], recv_sem=r3.at[b, o - 1],
                    device_id=(to, me_w), device_id_type=MESH,
                )
            )
        return out

    def wait3(b):
        for o in range(1, nr):
            frm = lax.rem(me_r + nr - o, nr)
            pltpu.make_async_remote_copy(
                src_ref=gs.at[rows_of(b, frm)],
                dst_ref=gs.at[rows_of(b, frm)],
                send_sem=s3.at[b, o - 1], recv_sem=r3.at[b, o - 1],
                device_id=(frm, me_w), device_id_type=MESH,
            ).wait_recv()

    def wait_sent(copies):
        for cp in copies:
            cp.wait_send()

    def wait_got(copies):
        for cp in copies:
            cp.wait_recv()

    def interior(fn, lo, hi):
        def body(m, carry):
            fn(m)
            return carry

        lax.fori_loop(lo, hi, body, 0, unroll=(hi - lo) // 2)

    def chain(j):
        n = 64 * j
        blocks = [gram_block(gs, scale, i, j) for i in range(j + 1)]
        schur = blocks[j]
        if j:
            known = inv_out[0:n, 0:n]
            above = mm(known, jnp.concatenate(blocks[:j], axis=0))
            schur = schur - mm(above, above, TN)
        r, m = factor(schur)
        col = r
        if j:
            inv_out[n : n + 64, 0:n] = -mm(m, mm(above, known, TN))
            col = jnp.concatenate([above, r], axis=0)
            bm[0 : n + 64, n - 64 : n] += col
        inv_out[n : n + 64, n : n + 64] = m
        bm[0 : n + 64, n : n + 64] = SHIFTS[j] * col

    halos = [halo(j) for j in range(STEPS)]
    z_copies = [
        pltpu.make_async_copy(vb[j].at[pl.ds(REACH, mil)], z_out.at[j], z_sem.at[j])
        for j in range(NBLK)
    ]
    first = [stage1(b) for b in range(3)]
    second = [stage2(b) for b in range(3)]
    third = [stage3(b) for b in range(3)]

    def forward1(b):
        wait_got(first[b])
        sum1(b)
        start_all(second[b])

    def forward2(b):
        wait2(b)
        sum2(b)
        start_all(third[b])

    def receive(j):
        wait_got(halos[j])
        vb[j][0:REACH] = hb[j, 0]
        vb[j][mil + REACH : mil + 2 * REACH] = hb[j, 1]

    def between(j, lo, hi):
        for m in list(range(lo, hi)) + list(range(mil - hi, mil - lo)):
            apply_one(j, m)

    def edges(j):
        between(j, 0, REACH)

    def inner(j, w):
        interior(functools.partial(apply_one, j), w, mil - w)

    def get_tiles():
        for cp in tile_copies:
            cp.wait()
        for cp in index_copies:
            cp.wait()

    def publish(j):
        z_copies[j].start()
        gram(j)
        if j > 1:
            start_all(first[j - 2])

    middle = mil // 2
    start_all(halos[0])
    interior(load_start, REACH, mil - REACH)
    publish(0)
    get_tiles()
    inner(0, REACH)
    inner(1, 2 * REACH)
    receive(0)
    edges(0)
    start_all(halos[1])
    between(1, REACH, 2 * REACH)
    publish(1)
    inner(2, 2 * REACH)
    receive(1)
    edges(1)
    start_all(halos[2])
    between(2, REACH, 2 * REACH)
    publish(2)
    inner(3, 2 * REACH)
    receive(2)
    edges(2)
    start_all(halos[3])
    publish(3)
    forward1(0)
    between(3, REACH, 2 * REACH)
    accumulate(STEPS, range(REACH, middle), True)
    accumulate(STEPS, range(middle, mil - REACH), False)
    receive(3)
    edges(3)
    z_copies[STEPS].start()
    accumulate(STEPS, list(range(REACH)) + list(range(mil - REACH, mil)), False)
    fold(STEPS)
    start_all(first[2])
    for j in range(STEPS):
        wait_sent(halos[j])
    forward1(1)
    forward2(0)
    forward1(2)
    forward2(1)
    wait3(0)
    chain(0)
    chain(1)
    forward2(2)
    chain(2)
    wait3(1)
    chain(3)
    for b in range(3):
        wait_sent(first[b])
        wait_sent(second[b])
    wait_sent(third[0])
    wait_sent(third[1])
    for cp in z_copies:
        cp.wait()
    wait3(2)
    s_out[...] = gs[BATCHES[2][0] :]
    wait_sent(third[2])


def finish_kernel(scale, s_ref, inv_ref, bm_ref, z_hbm, q_ref, h_ref, zb, sems):
    mil = zb.shape[1]
    copies = [pltpu.make_async_copy(z_hbm.at[k], zb.at[k], sems.at[k]) for k in range(NBLK)]
    for cp in copies:
        cp.start()

    n = 64 * STEPS
    blocks = [gram_block(s_ref, scale, i, STEPS, BATCHES[2][0]) for i in range(NBLK)]
    known = inv_ref[...]
    above = mm(known, jnp.concatenate(blocks[:STEPS], axis=0))
    r, m = factor(blocks[STEPS] - mm(above, above, TN))
    row = -mm(m, mm(above, known, TN))
    coef = []
    for k in range(NBLK):
        c = m
        if k < STEPS:
            c = row[:, 128 * (k // 2) : 128 * (k // 2) + 128]
            if k % 2:
                c = pltpu.roll(c, 64, 1)
            c = c[:, :64]
        hi = c.astype(BF16)
        lo = (c - hi.astype(F32)).astype(BF16)
        coef.append(
            jnp.concatenate(
                [jnp.concatenate([hi, hi], axis=1), jnp.concatenate([lo, lo], axis=1)], axis=0
            )
        )
    coef = jnp.concatenate(coef, axis=1)

    corner = pltpu.roll(inv_ref[n - 64 : n, n - 128 : n], 64, 1)[:, :64]
    known_h = mm(bm_ref[...], known, NT)
    h_ref[:, 0 : n - 64] = known_h[:, 0 : n - 64]
    h_ref[:, n - 64 : n] = known_h[:, n - 64 : n] + mm(
        jnp.concatenate([above, r], axis=0), corner, NT
    )

    for cp in copies:
        cp.wait()

    def body(g, carry):
        right = jnp.concatenate(
            [jnp.concatenate([zb[k, 2 * g], zb[k, 2 * g + 1]], axis=1) for k in range(NBLK)],
            axis=0,
        )
        prod = lax.dot_general(coef, right, NN, preferred_element_type=F32)
        q_ref[:, pl.ds(pl.multiple_of(g * 256, 256), 256)] = prod[:64] + prod[64:]
        return carry

    lax.fori_loop(0, mil // 2, body, 0, unroll=8)


def in_hbm(*arrays):
    return [pltpu.with_memory_space_constraint(a, pltpu.HBM) for a in arrays]


def on_device(nr, nw, kernel_tiles, neighbours, tile_counts, start_block):
    mil, slots, states = kernel_tiles.shape[:3]
    width = start_block.shape[1]
    rows = mil * states
    scale = 1.0 / (rows * nr * nw)
    vmem = pl.BlockSpec(memory_space=pltpu.VMEM)
    hbm = pl.BlockSpec(memory_space=pltpu.HBM)
    size = 256 // nr
    square = STEPS * width
    dma = pltpu.SemaphoreType.DMA
    vec = pltpu.VMEM((mil + 2 * REACH + 1, 2 * width, states), BF16)
    packed, inv, part, z = pl.pallas_call(
        functools.partial(krylov_kernel, nr, nw, scale),
        out_shape=(
            jax.ShapeDtypeStruct((256, 128), F32),
            jax.ShapeDtypeStruct((square, square), F32),
            jax.ShapeDtypeStruct((NBLK * width, square), F32),
            jax.ShapeDtypeStruct((NBLK, mil, 2 * width, states), BF16),
        ),
        in_specs=[hbm, hbm, hbm, hbm],
        out_specs=(vmem, vmem, vmem, hbm),
        scratch_shapes=[
            pltpu.SMEM((slots, mil), jnp.int32),
            pltpu.SMEM((mil,), jnp.int32),
            pltpu.VMEM((mil, slots, states, states), BF16),
            pltpu.VMEM((width, rows), F32),
            vec, vec, vec, vec, vec,
            pltpu.VMEM((2, 16, 128), BF16),
            pltpu.VMEM((mil, 8, 128), F32),
            pltpu.VMEM((STEPS, 2, REACH, 2 * width, states), BF16),
            pltpu.VMEM((NBLK * 128, 128), F32),
            pltpu.VMEM((GRAM_ROWS, 128), F32),
            pltpu.VMEM((3, nr, size, 128), F32),
            pltpu.VMEM((3, size, 128), F32),
            pltpu.VMEM((3, nw, size, 128), F32),
            pltpu.VMEM((GRAM_ROWS, 128), F32),
            dma((7,)), dma((NBLK,)),
            dma((STEPS, 2)), dma((STEPS, 2)),
            dma((3, nr)), dma((3, nr)),
            dma((3, nw)), dma((3, nw)),
            dma((3, nr)), dma((3, nr)),
        ],
        compiler_params=pltpu.CompilerParams(
            collective_id=0, has_side_effects=True, vmem_limit_bytes=40 * 1024 * 1024
        ),
    )(*in_hbm(neighbours.T, tile_counts, kernel_tiles, start_block.T))
    last, hess = pl.pallas_call(
        functools.partial(finish_kernel, scale),
        out_shape=(
            jax.ShapeDtypeStruct((width, rows), F32),
            jax.ShapeDtypeStruct((NBLK * width, square), F32),
        ),
        in_specs=[vmem, vmem, vmem, hbm],
        out_specs=(vmem, vmem),
        scratch_shapes=[
            pltpu.VMEM((NBLK, mil, 2 * width, states), BF16),
            dma((NBLK,)),
        ],
        compiler_params=pltpu.CompilerParams(vmem_limit_bytes=40 * 1024 * 1024),
    )(packed, inv, part, z)
    return last.T, hess


def solution(mesh):
    nr, nw = mesh.shape["region"], mesh.shape["within"]
    return jax.shard_map(
        functools.partial(on_device, nr, nw),
        mesh=mesh,
        in_specs=(
            P(("region", "within"), None, None, None),
            P(("region", "within"), None),
            P(("region", "within")),
            P(("region", "within"), None),
        ),
        out_specs=(P(("region", "within"), None), P()),
        check_vma=False,
    )
```

```python
import functools

import jax
import jax.numpy as jnp
from jax import lax
from jax.experimental import pallas as pl
from jax.experimental.pallas import tpu as pltpu
from jax.sharding import PartitionSpec as P

REACH = 2
STEPS = 4
NBLK = STEPS + 1
SHIFTS = (0.0, 0.5, 1.0, 0.25)
F32 = jnp.float32
BF16 = jnp.bfloat16
MESH = pl.DeviceIdType.MESH
HIGHEST = lax.Precision.HIGHEST
NT = (((1,), (1,)), ((), ()))
TN = (((0,), (0,)), ((), ()))
NN = (((1,), (0,)), ((), ()))
BATCHES = ((0, 256), (256, 128), (384, 256))
GRAM_ROWS = 640

def place(i, j):
    t = i + (j * (j + 1) // 2 if j < 3 else 0)
    return BATCHES[max(j - 2, 0)][0] + (t // 2) * 64, t % 2


def split(x):
    hi = x.astype(BF16)
    lo = (x - hi.astype(F32)).astype(BF16)
    return jnp.concatenate([hi, lo], axis=0)


def mm(a, b, dims=NN):
    return lax.dot_general(a, b, dims, precision=HIGHEST, preferred_element_type=F32)


def gram_block(ref, scale, i, j, first=0):
    row, odd = place(i, j)
    x = ref[row - first : row - first + 64]
    if odd:
        x = pltpu.roll(x, 64, 1)
    return x[:, :64] * scale


def factor(block):
    size = block.shape[0]
    eye = (
        lax.broadcasted_iota(jnp.int32, (size, size), 0)
        == lax.broadcasted_iota(jnp.int32, (size, size), 1)
    ).astype(F32)
    cur = jnp.concatenate([block, eye], axis=1)
    done = []
    for kb in range(size // 8):
        n = size - 8 * kb
        rid = lax.broadcasted_iota(jnp.int32, (n, 128), 0)
        cols = [
            jnp.broadcast_to(cur[:, 8 * kb + p : 8 * kb + p + 1], (n, 128)) for p in range(8)
        ]
        scale = jnp.zeros((8, 128), F32)
        for p in range(0, 8, 2):
            a, b, c = cols[p][p : p + 1], cols[p][p + 1 : p + 2], cols[p + 1][p + 1 : p + 2]
            det = a * c - b * b
            inv_a = 1.0 / a
            inv_c = a * (1.0 / det)
            ratio = b * inv_a
            scale = jnp.where(rid[:8] == p, lax.rsqrt(a), scale)
            scale = jnp.where(rid[:8] == p + 1, lax.rsqrt(det * inv_a), scale)
            mult0 = jnp.where(rid > p, cols[p] * inv_a, 0.0)
            mult1 = jnp.where(rid > p + 1, (cols[p + 1] - mult0 * b) * inv_c, 0.0)
            row0 = cur[p : p + 1]
            row1 = cur[p + 1 : p + 2] - ratio * row0
            cur = cur - mult0 * row0 - mult1 * row1
            for q in range(p + 2, 8):
                q0 = cols[q][p : p + 1]
                q1 = cols[q][p + 1 : p + 2] - ratio * q0
                cols[q] = cols[q] - mult0 * q0 - mult1 * q1
        done.append(cur[:8] * scale)
        cur = cur[8:]
    full = jnp.concatenate(done, axis=0)
    upper = lax.broadcasted_iota(jnp.int32, (size, size), 0) <= lax.broadcasted_iota(
        jnp.int32, (size, size), 1
    )
    r = jnp.where(upper, full[:, :size], 0.0)
    m = pltpu.roll(full, size, 1)[:, :size]
    return r, m


def krylov_kernel(
    nr, nw, scale, nbr_hbm, cnt_hbm, tiles, start, s_out, inv_out, bm, z_out,
    nbr, cnt, tl, x0, v0, v1, v2, v3, v4, ones, irs, hb, acc, gb, land1, part, land2, gs,
    in_sem, z_sem, hs, hr, s1, r1, s2, r2, s3, r3,
):
    vb = (v0, v1, v2, v3, v4)
    mil = z_out.shape[1]
    slots = tl.shape[1]
    zero_at = mil + 2 * REACH
    n = nr * nw
    me_r = lax.axis_index("region")
    me_w = lax.axis_index("within")
    me = me_r * nw + me_w
    base = me * mil
    right = lax.rem(me + 1, n)
    left = lax.rem(me + n - 1, n)
    right_id = (right // nw, lax.rem(right, nw))
    left_id = (left // nw, lax.rem(left, nw))

    barrier = pltpu.get_barrier_semaphore()
    for o in range(1, nr):
        pl.semaphore_signal(
            barrier, inc=1, device_id=(lax.rem(me_r + o, nr), me_w), device_id_type=MESH
        )
    for o in range(1, nw):
        pl.semaphore_signal(
            barrier, inc=1, device_id=(me_r, lax.rem(me_w + o, nw)), device_id_type=MESH
        )
    pl.semaphore_signal(barrier, inc=1, device_id=right_id, device_id_type=MESH)
    pl.semaphore_signal(barrier, inc=1, device_id=left_id, device_id_type=MESH)

    start_copy = pltpu.make_async_copy(start, x0, in_sem.at[0])
    start_copy.start()
    index_copies = (
        pltpu.make_async_copy(nbr_hbm, nbr, in_sem.at[5]),
        pltpu.make_async_copy(cnt_hbm, cnt, in_sem.at[6]),
    )
    for cp in index_copies:
        cp.start()
    part_mil = mil // 4
    tile_copies = []
    for c in range(4):
        cp = pltpu.make_async_copy(
            tiles.at[pl.ds(c * part_mil, part_mil)],
            tl.at[pl.ds(c * part_mil, part_mil)],
            in_sem.at[1 + c],
        )
        cp.start()
        tile_copies.append(cp)

    for j in range(STEPS):
        vb[j][zero_at] = jnp.zeros((128, 128), BF16)
    ones[0] = jnp.ones((16, 128), BF16)
    ones[1] = jnp.zeros((16, 128), BF16)
    for row in (192, GRAM_ROWS - 64):
        gb[row : row + 64] = jnp.zeros((64, 128), F32)
    inv_out[...] = jnp.zeros(inv_out.shape, F32)
    bm[...] = jnp.zeros(bm.shape, F32)

    start_copy.wait()

    def load_start(m):
        lanes = pl.ds(pl.multiple_of(m * 128, 128), 128)
        vb[0][m + REACH] = split(x0[:, lanes])

    for m in list(range(REACH)) + list(range(mil - REACH, mil)):
        load_start(m)
    pl.semaphore_wait(barrier, nr + nw)

    def halo(j):
        return (
            pltpu.make_async_remote_copy(
                src_ref=vb[j].at[pl.ds(mil, REACH)], dst_ref=hb.at[j, 0],
                send_sem=hs.at[j, 0], recv_sem=hr.at[j, 0],
                device_id=right_id, device_id_type=MESH,
            ),
            pltpu.make_async_remote_copy(
                src_ref=vb[j].at[pl.ds(REACH, REACH)], dst_ref=hb.at[j, 1],
                send_sem=hs.at[j, 1], recv_sem=hr.at[j, 1],
                device_id=left_id, device_id_type=MESH,
            ),
        )

    def start_all(copies):
        for cp in copies:
            cp.start()

    def apply_one(j, m):
        vs, tiles_m = [], []
        for k in range(slots):
            live = k < cnt[m]
            at = jnp.where(live, nbr[k, m] - base + REACH, zero_at)
            v = vb[j][at]
            if j == 0:
                v = jnp.concatenate([v, ones[jnp.where(live, 0, 1)]], axis=0)
            vs.append(v)
            tiles_m.append(tl[m, k])
        prod = lax.dot_general(
            jnp.concatenate(vs, axis=1), jnp.concatenate(tiles_m, axis=1), NT,
            preferred_element_type=F32,
        )
        if j == 0:
            inv = 1.0 / prod[128:136]
            irs[m] = inv
        else:
            inv = irs[m]
        w = (prod[:64] + prod[64:128]) * inv[0:1]
        if SHIFTS[j] != 0.0:
            own = vb[j][m + REACH].astype(F32)
            w = w - SHIFTS[j] * (own[:64] + own[64:])
        vb[j + 1][m + REACH] = split(w)

    def accumulate(j, milestones, fresh):
        rows = (j + 1) * 128
        stack = [
            jnp.concatenate([vb[i][REACH + m] for m in milestones], axis=1) for i in range(j + 1)
        ]
        prod = lax.dot_general(
            jnp.concatenate(stack, axis=0), stack[j], NT, preferred_element_type=F32
        )
        if fresh:
            acc[:rows] = prod
        else:
            acc[:rows] += prod

    def gram(j):
        accumulate(j, range(mil // 2), True)
        accumulate(j, range(mil // 2, mil), False)
        fold(j)

    def fold(j):
        lane = lax.broadcasted_iota(jnp.int32, (64, 128), 1)
        for i in range(j + 1):
            blk = acc[i * 128 : i * 128 + 64] + acc[i * 128 + 64 : i * 128 + 128]
            blk = blk + pltpu.roll(blk, 64, 1)
            row, odd = place(i, j)
            if odd:
                gb[row : row + 64] = jnp.where(lane < 64, gb[row : row + 64], blk)
            else:
                gb[row : row + 64] = blk

    def rows_of(b, c):
        first, total = BATCHES[b]
        size = total // nr
        return pl.ds(pl.multiple_of(first + c * size, 8), size)

    def stage1(b):
        size = BATCHES[b][1] // nr
        out = []
        for o in range(1, nr):
            to = lax.rem(me_r + o, nr)
            out.append(
                pltpu.make_async_remote_copy(
                    src_ref=gb.at[rows_of(b, to)],
                    dst_ref=land1.at[b, o - 1, pl.ds(0, size)],
                    send_sem=s1.at[b, o - 1], recv_sem=r1.at[b, o - 1],
                    device_id=(to, me_w), device_id_type=MESH,
                )
            )
        return out

    def sum1(b):
        size = BATCHES[b][1] // nr
        total = gb[rows_of(b, me_r)]
        for o in range(1, nr):
            total = total + land1[b, o - 1, 0:size]
        part[b, 0:size] = total
        land2[b, me_w, 0:size] = total

    def stage2(b):
        size = BATCHES[b][1] // nr
        out = []
        for o in range(1, nw):
            to = lax.rem(me_w + o, nw)
            out.append(
                pltpu.make_async_remote_copy(
                    src_ref=part.at[b, pl.ds(0, size)],
                    dst_ref=land2.at[b, me_w, pl.ds(0, size)],
                    send_sem=s2.at[b, o - 1], recv_sem=r2.at[b, o - 1],
                    device_id=(me_r, to), device_id_type=MESH,
                )
            )
        return out

    def wait2(b):
        size = BATCHES[b][1] // nr
        for o in range(1, nw):
            frm = lax.rem(me_w + nw - o, nw)
            pltpu.make_async_remote_copy(
                src_ref=part.at[b, pl.ds(0, size)],
                dst_ref=land2.at[b, frm, pl.ds(0, size)],
                send_sem=s2.at[b, o - 1], recv_sem=r2.at[b, o - 1],
                device_id=(me_r, frm), device_id_type=MESH,
            ).wait_recv()

    def sum2(b):
        size = BATCHES[b][1] // nr
        total = land2[b, 0, 0:size]
        for i in range(1, nw):
            total = total + land2[b, i, 0:size]
        gs[rows_of(b, me_r)] = total

    def stage3(b):
        out = []
        for o in range(1, nr):
            to = lax.rem(me_r + o, nr)
            out.append(
                pltpu.make_async_remote_copy(
                    src_ref=gs.at[rows_of(b, me_r)],
                    dst_ref=gs.at[rows_of(b, me_r)],
                    send_sem=s3.at[b, o - 1], recv_sem=r3.at[b, o - 1],
                    device_id=(to, me_w), device_id_type=MESH,
                )
            )
        return out

    def wait3(b):
        for o in range(1, nr):
            frm = lax.rem(me_r + nr - o, nr)
            pltpu.make_async_remote_copy(
                src_ref=gs.at[rows_of(b, frm)],
                dst_ref=gs.at[rows_of(b, frm)],
                send_sem=s3.at[b, o - 1], recv_sem=r3.at[b, o - 1],
                device_id=(frm, me_w), device_id_type=MESH,
            ).wait_recv()

    def wait_sent(copies):
        for cp in copies:
            cp.wait_send()

    def wait_got(copies):
        for cp in copies:
            cp.wait_recv()

    def interior(fn, lo, hi):
        def body(m, carry):
            fn(m)
            return carry

        lax.fori_loop(lo, hi, body, 0, unroll=(hi - lo) // 2)

    def chain(j):
        n = 64 * j
        blocks = [gram_block(gs, scale, i, j) for i in range(j + 1)]
        schur = blocks[j]
        if j:
            known = inv_out[0:n, 0:n]
            above = mm(known, jnp.concatenate(blocks[:j], axis=0))
            schur = schur - mm(above, above, TN)
        r, m = factor(schur)
        col = r
        if j:
            inv_out[n : n + 64, 0:n] = -mm(m, mm(above, known, TN))
            col = jnp.concatenate([above, r], axis=0)
            bm[0 : n + 64, n - 64 : n] += col
        inv_out[n : n + 64, n : n + 64] = m
        bm[0 : n + 64, n : n + 64] = SHIFTS[j] * col

    halos = [halo(j) for j in range(STEPS)]
    z_copies = [
        pltpu.make_async_copy(vb[j].at[pl.ds(REACH, mil)], z_out.at[j], z_sem.at[j])
        for j in range(NBLK)
    ]
    first = [stage1(b) for b in range(3)]
    second = [stage2(b) for b in range(3)]
    third = [stage3(b) for b in range(3)]

    def forward1(b):
        wait_got(first[b])
        sum1(b)
        start_all(second[b])

    def forward2(b):
        wait2(b)
        sum2(b)
        start_all(third[b])

    def receive(j):
        wait_got(halos[j])
        vb[j][0:REACH] = hb[j, 0]
        vb[j][mil + REACH : mil + 2 * REACH] = hb[j, 1]

    def between(j, lo, hi):
        for m in list(range(lo, hi)) + list(range(mil - hi, mil - lo)):
            apply_one(j, m)

    def edges(j):
        between(j, 0, REACH)

    def inner(j, w):
        interior(functools.partial(apply_one, j), w, mil - w)

    def get_tiles():
        for cp in tile_copies:
            cp.wait()
        for cp in index_copies:
            cp.wait()

    def publish(j):
        z_copies[j].start()
        gram(j)
        if j > 1:
            start_all(first[j - 2])

    middle = mil // 2
    start_all(halos[0])
    interior(load_start, REACH, mil - REACH)
    publish(0)
    get_tiles()
    inner(0, REACH)
    inner(1, 2 * REACH)
    receive(0)
    edges(0)
    start_all(halos[1])
    between(1, REACH, 2 * REACH)
    publish(1)
    inner(2, 2 * REACH)
    receive(1)
    edges(1)
    start_all(halos[2])
    between(2, REACH, 2 * REACH)
    publish(2)
    inner(3, 2 * REACH)
    receive(2)
    edges(2)
    start_all(halos[3])
    publish(3)
    forward1(0)
    between(3, REACH, 2 * REACH)
    accumulate(STEPS, range(REACH, middle), True)
    accumulate(STEPS, range(middle, mil - REACH), False)
    receive(3)
    edges(3)
    z_copies[STEPS].start()
    accumulate(STEPS, list(range(REACH)) + list(range(mil - REACH, mil)), False)
    fold(STEPS)
    start_all(first[2])
    for j in range(STEPS):
        wait_sent(halos[j])
    forward1(1)
    forward2(0)
    forward1(2)
    forward2(1)
    wait3(0)
    chain(0)
    chain(1)
    forward2(2)
    chain(2)
    wait3(1)
    chain(3)
    for b in range(3):
        wait_sent(first[b])
        wait_sent(second[b])
    wait_sent(third[0])
    wait_sent(third[1])
    for cp in z_copies:
        cp.wait()
    wait3(2)
    s_out[...] = gs[BATCHES[2][0] :]
    wait_sent(third[2])


def finish_kernel(scale, s_ref, inv_ref, bm_ref, z_hbm, q_hbm, h_ref, zb, q_ref, sems, out_sems):
    mil = zb.shape[1]
    copies = [pltpu.make_async_copy(z_hbm.at[k], zb.at[k], sems.at[k]) for k in range(NBLK)]
    for cp in copies:
        cp.start()

    n = 64 * STEPS
    blocks = [gram_block(s_ref, scale, i, STEPS, BATCHES[2][0]) for i in range(NBLK)]
    known = inv_ref[...]
    above = mm(known, jnp.concatenate(blocks[:STEPS], axis=0))
    r, m = factor(blocks[STEPS] - mm(above, above, TN))
    row = -mm(m, mm(above, known, TN))
    coef = []
    for k in range(NBLK):
        c = m
        if k < STEPS:
            c = row[:, 128 * (k // 2) : 128 * (k // 2) + 128]
            if k % 2:
                c = pltpu.roll(c, 64, 1)
            c = c[:, :64]
        hi = c.astype(BF16)
        lo = (c - hi.astype(F32)).astype(BF16)
        coef.append(
            jnp.concatenate(
                [jnp.concatenate([hi, hi], axis=1), jnp.concatenate([lo, lo], axis=1)], axis=0
            )
        )
    coef = jnp.concatenate(coef, axis=1)

    corner = pltpu.roll(inv_ref[n - 64 : n, n - 128 : n], 64, 1)[:, :64]
    known_h = mm(bm_ref[...], known, NT)
    h_ref[:, 0 : n - 64] = known_h[:, 0 : n - 64]
    h_ref[:, n - 64 : n] = known_h[:, n - 64 : n] + mm(
        jnp.concatenate([above, r], axis=0), corner, NT
    )

    for cp in copies:
        cp.wait()

    def body(g, carry):
        right = jnp.concatenate(
            [jnp.concatenate([zb[k, 2 * g], zb[k, 2 * g + 1]], axis=1) for k in range(NBLK)],
            axis=0,
        )
        prod = lax.dot_general(coef, right, NN, preferred_element_type=F32)
        q_ref[:, pl.ds(pl.multiple_of(g * 256, 256), 256)] = prod[:64] + prod[64:]
        return carry

    quarter = mil // 8
    outs = []
    for c in range(4):
        lax.fori_loop(c * quarter, (c + 1) * quarter, body, 0, unroll=quarter)
        lanes = pl.ds(c * quarter * 256, quarter * 256)
        out = pltpu.make_async_copy(q_ref.at[:, lanes], q_hbm.at[:, lanes], out_sems.at[c])
        out.start()
        outs.append(out)
    for out in outs:
        out.wait()


def in_hbm(*arrays):
    return [pltpu.with_memory_space_constraint(a, pltpu.HBM) for a in arrays]


def on_device(nr, nw, kernel_tiles, neighbours, tile_counts, start_block):
    mil, slots, states = kernel_tiles.shape[:3]
    width = start_block.shape[1]
    rows = mil * states
    scale = 1.0 / (rows * nr * nw)
    vmem = pl.BlockSpec(memory_space=pltpu.VMEM)
    hbm = pl.BlockSpec(memory_space=pltpu.HBM)
    size = 256 // nr
    square = STEPS * width
    dma = pltpu.SemaphoreType.DMA
    vec = pltpu.VMEM((mil + 2 * REACH + 1, 2 * width, states), BF16)
    packed, inv, part, z = pl.pallas_call(
        functools.partial(krylov_kernel, nr, nw, scale),
        out_shape=(
            jax.ShapeDtypeStruct((256, 128), F32),
            jax.ShapeDtypeStruct((square, square), F32),
            jax.ShapeDtypeStruct((NBLK * width, square), F32),
            jax.ShapeDtypeStruct((NBLK, mil, 2 * width, states), BF16),
        ),
        in_specs=[hbm, hbm, hbm, hbm],
        out_specs=(vmem, vmem, vmem, hbm),
        scratch_shapes=[
            pltpu.SMEM((slots, mil), jnp.int32),
            pltpu.SMEM((mil,), jnp.int32),
            pltpu.VMEM((mil, slots, states, states), BF16),
            pltpu.VMEM((width, rows), F32),
            vec, vec, vec, vec, vec,
            pltpu.VMEM((2, 16, 128), BF16),
            pltpu.VMEM((mil, 8, 128), F32),
            pltpu.VMEM((STEPS, 2, REACH, 2 * width, states), BF16),
            pltpu.VMEM((NBLK * 128, 128), F32),
            pltpu.VMEM((GRAM_ROWS, 128), F32),
            pltpu.VMEM((3, nr, size, 128), F32),
            pltpu.VMEM((3, size, 128), F32),
            pltpu.VMEM((3, nw, size, 128), F32),
            pltpu.VMEM((GRAM_ROWS, 128), F32),
            dma((7,)), dma((NBLK,)),
            dma((STEPS, 2)), dma((STEPS, 2)),
            dma((3, nr)), dma((3, nr)),
            dma((3, nw)), dma((3, nw)),
            dma((3, nr)), dma((3, nr)),
        ],
        compiler_params=pltpu.CompilerParams(
            collective_id=0, has_side_effects=True, vmem_limit_bytes=40 * 1024 * 1024
        ),
    )(*in_hbm(neighbours.T, tile_counts, kernel_tiles, start_block.T))
    last, hess = pl.pallas_call(
        functools.partial(finish_kernel, scale),
        out_shape=(
            jax.ShapeDtypeStruct((width, rows), F32),
            jax.ShapeDtypeStruct((NBLK * width, square), F32),
        ),
        in_specs=[vmem, vmem, vmem, hbm],
        out_specs=(hbm, vmem),
        scratch_shapes=[
            pltpu.VMEM((NBLK, mil, 2 * width, states), BF16),
            pltpu.VMEM((width, rows), F32),
            dma((NBLK,)),
            dma((4,)),
        ],
        compiler_params=pltpu.CompilerParams(vmem_limit_bytes=40 * 1024 * 1024),
    )(packed, inv, part, z)
    return last.T, hess


def solution(mesh):
    nr, nw = mesh.shape["region"], mesh.shape["within"]
    return jax.shard_map(
        functools.partial(on_device, nr, nw),
        mesh=mesh,
        in_specs=(
            P(("region", "within"), None, None, None),
            P(("region", "within"), None),
            P(("region", "within")),
            P(("region", "within"), None),
        ),
        out_specs=(P(("region", "within"), None), P()),
        check_vma=False,
    )
```
